32 devices in a mesh: gx: 4 (over y, core), gy: 8 (over z, x).
Axes of the slice: x: 2, y: 2, z: 4, core: 2. Of those that a mesh axis runs over, the one named last changes fastest.
Arguments:
- rhs: float32 [32, 64, 512], P('gx', 'gy'), may hold values from -18 to 18
- diag: float32 [32, 64, 512], P('gx', 'gy'), may hold values from 0.5 to 2
- smoother_center: float32 [32, 64, 512], P('gx', 'gy'), may hold values from 0.1 to 0.2
- smoother_faces: float32 [6, 32, 64, 512], P(None, 'gx', 'gy'), may hold values from 0.01 to 0.05
- send_count: int32 [4, 8, 8], P('gx', 'gy'), may hold values from 0 to 4096, as said below
- send_cell: int32 [4, 8, 8, 4096], P('gx', 'gy'), may hold values from 0 to 32767, as said below
- restrict_col: int32 [27, 4, 8, 4096], P(None, 'gx', 'gy'), may hold values from 0 to 65535, as said below
- restrict_vals: float32 [27, 4, 8, 4096], P(None, 'gx', 'gy'), may hold values from 0.03 to 0.2
- coarse_col: int32 [16, 4, 8, 4096], P(None, 'gx', 'gy'), may hold values from 0 to 12287, as said below
- coarse_diag: float32 [4, 8, 4096], P('gx', 'gy'), may hold values from 3 to 6
- coarse_vals: float32 [16, 4, 8, 4096], P(None, 'gx', 'gy'), may hold values from -3 to 3
- csmooth_diag: float32 [4, 8, 4096], P('gx', 'gy'), may hold values from 0.15 to 0.3
- csmooth_vals: float32 [16, 4, 8, 4096], P(None, 'gx', 'gy'), may hold values from -0.3 to 0.3
- remote_row: int32 [4, 4, 8, 8, 4096], P(None, 'gx', 'gy'), may hold values from 0 to 4095, as said below
- remote_vals: float32 [4, 4, 8, 8, 4096], P(None, 'gx', 'gy'), may hold values from 0.3 to 1
- interp_row: int32 [4, 32, 64, 512], P(None, 'gx', 'gy'), may hold values from 0 to 4095, as said below
- interp_vals: float32 [4, 32, 64, 512], P(None, 'gx', 'gy'), may hold values from 0.3 to 1
Outputs:
- solution: float32 [32, 64, 512], P('gx', 'gy')
- residual: float32 [32, 64, 512], P('gx', 'gy')
The draws below stay inside these ranges and needn't reach their ends.
Inputs may be any that keep to these rules, and one draw needn't show every extreme that they name: `send_count`: zero towards a neighbour outside the grid; one device receives 4096 used slots from each of its eight neighbours, and about a quarter of the devices receive several times more than the rest. `send_cell`: the cell of a slot towards direction d lies within 2 cells of the side facing that neighbour, within 4 cells of both sides for a diagonal neighbour. The slots of one direction in one aligned block of 128 slots lie in one run of 128 cells along z that starts at a multiple of 128. `restrict_col`: only a device's first 1024 coarse rows read received slots. For one k, the entries of one aligned block of 128 coarse rows lie in one aligned block of 128 columns. `coarse_col`: only a device's first 1024 coarse rows read neighbours' rows. For one k, the entries of one aligned block of 128 coarse rows lie in one aligned block of 128 columns. `remote_row`: for one k and one direction, the entries of one aligned block of 128 slots lie in one aligned block of 128 coarse rows. `interp_row`: for one k, the entries of one run of 128 cells along z that starts at a multiple of 128 lie in one aligned block of 128 coarse rows.
All inputs are finite; a program needn't handle non-finite values.
Results may differ from the reference program's by a relative error of at most 0.0003.
Values sent between devices are 32-bit elements; how exact they have to be, the bound alone decides.
A program may use at most 128 MiB of HBM per device.

```python
import jax
import jax.numpy as jnp

CX = 8
CY = 8
NZ = 512
CAP = 4096
BLK = 128
KR = 27
KI = 4
KA = 16
NX = 32
NY = 64
NCD = 4096
NRIM = 1024
N_GX = 4
N_GY = 8
DEVICES = 32


OFFSET_X = (-1, -1, -1, 0, 0, 1, 1, 1)


OFFSET_Y = (-1, 0, 1, -1, 1, -1, 0, 1)


def draw_send_count(key, part):
    key_heavy_x, key_heavy_y, key_busy, key_lower, key_upper = jax.random.split(jax.random.fold_in(key, 7), 5)
    heavy_x = jax.random.randint(key_heavy_x, (), 1, N_GX - 1)
    heavy_y = jax.random.randint(key_heavy_y, (), 1, N_GY - 1)
    is_busy = jax.random.randint(key_busy, (N_GX + 2, N_GY + 2), 0, 4) == 0
    step_x = jnp.array(OFFSET_X, jnp.int32)[None, None, :]
    step_y = jnp.array(OFFSET_Y, jnp.int32)[None, None, :]
    dest_x = jnp.arange(N_GX, dtype=jnp.int32)[:, None, None] + step_x
    dest_y = jnp.arange(N_GY, dtype=jnp.int32)[None, :, None] + step_y
    exists = (dest_x >= 0) & (dest_x < N_GX) & (dest_y >= 0) & (dest_y < N_GY)
    low_counts = jax.random.randint(key_lower, (N_GX, N_GY, 8), max(1, CAP // 6), CAP // 3 + 1)
    high_counts = jax.random.randint(key_upper, (N_GX, N_GY, 8), CAP // 2, CAP + 1)
    counts = jnp.where(is_busy[dest_x + 1, dest_y + 1], high_counts, low_counts)
    counts = jnp.where((dest_x == heavy_x) & (dest_y == heavy_y), CAP, counts)
    counts = jnp.where(exists, counts, 0)
    return counts.astype(jnp.int32)


def draw_send_cell(key, part):
    key_x, key_y, key_z, key_off = jax.random.split(jax.random.fold_in(key, 11), 4)
    step_x = jnp.array(OFFSET_X, jnp.int32)[None, None, :, None]
    step_y = jnp.array(OFFSET_Y, jnp.int32)[None, None, :, None]
    band_width = jnp.where((step_x != 0) & (step_y != 0), 4, 2)
    low_x = jnp.where(step_x == 1, CX - band_width, 0)
    high_x = jnp.where(step_x == -1, band_width, CX)
    low_y = jnp.where(step_y == 1, CY - band_width, 0)
    high_y = jnp.where(step_y == -1, band_width, CY)
    block_shape = (N_GX, N_GY, 8, CAP // BLK)
    cell_x = jax.random.randint(key_x, block_shape, low_x, high_x)
    cell_y = jax.random.randint(key_y, block_shape, low_y, high_y)
    z_block = jax.random.randint(key_z, block_shape, 0, NZ // BLK)
    offset = jax.random.randint(key_off, block_shape + (BLK,), 0, BLK)
    start = (cell_x * CY + cell_y) * NZ + z_block * BLK
    return (start[..., None] + offset).reshape(N_GX, N_GY, 8, CAP).astype(jnp.int32)


def blocked_columns(key, lead_shape, row_blocks, rim_blocks, near_blocks, far_blocks):
    key_far, key_near, key_pick, key_off = jax.random.split(key, 4)
    block_shape = lead_shape + (row_blocks,)
    block_ids = jnp.arange(row_blocks, dtype=jnp.int32)
    is_far = (jax.random.randint(key_far, block_shape, 0, 2) == 1) & (block_ids < rim_blocks)
    near_base = jax.random.randint(key_near, block_shape, 0, near_blocks)
    far_base = near_blocks + jax.random.randint(key_pick, block_shape, 0, far_blocks)
    base = jnp.where(is_far, far_base, near_base)
    offset = jax.random.randint(key_off, block_shape + (BLK,), 0, BLK)
    return (base[..., None] * BLK + offset).reshape(lead_shape + (row_blocks * BLK,)).astype(jnp.int32)


def draw_restrict_col(key, part):
    return blocked_columns(jax.random.fold_in(key, 13), (KR, N_GX, N_GY), NCD // BLK, NRIM // BLK, CX * CY * NZ // BLK, 8 * CAP // BLK)


def draw_coarse_col(key, part):
    return blocked_columns(jax.random.fold_in(key, 17), (KA, N_GX, N_GY), NCD // BLK, NRIM // BLK, NCD // BLK, 8 * NRIM // BLK)


def draw_remote_row(key, part):
    return blocked_columns(jax.random.fold_in(key, 19), (KI, N_GX, N_GY, 8), CAP // BLK, 0, NCD // BLK, 1)


def draw_interp_row(key, part):
    return blocked_columns(jax.random.fold_in(key, 23), (KI, NX, NY), NZ // BLK, 0, NCD // BLK, 1)


def block_scale(own_key, extent, cuts, smallest, high):
    level, own = 1.0, jax.random.fold_in(own_key, 6)
    for position, blocks in cuts:
        draws = jnp.exp(jax.random.uniform(jax.random.fold_in(own, position), (blocks,), jnp.float32, smallest / len(cuts), high / len(cuts)))
        level = level * jnp.repeat(draws, extent[position] // blocks).reshape([-1 if axis == position else 1 for axis in range(len(extent))])
    return level


def centred(own_key, extent, scale, most, cuts=(), kind=jnp.bfloat16):
    loudness = block_scale(own_key, extent, cuts, -0.22, 0.18) if cuts else 1.0
    values = jax.random.normal(own_key, extent, jnp.float32) * scale * loudness
    return jnp.minimum(jnp.maximum(values, -most), most).astype(kind)


def setup_inputs(seed: int = 0) -> dict:
    splits = jax.random.split(jax.random.key(seed), 18)
    return {
        "rhs": centred(splits[0], (NX, NY, NZ), 3.0, 18.0, ((0, 4), (1, 8)), jnp.float32),
        "diag": jnp.clip(0.5 + 1.5 * jax.random.uniform(splits[1], (NX, NY, NZ), jnp.float32) ** block_scale(splits[1], (NX, NY, NZ), ((0, 4), (1, 8)), -0.2, 0.2), 0.5, 2.0),
        "smoother_center": jnp.clip(0.1 + 0.1 * jax.random.uniform(splits[2], (NX, NY, NZ), jnp.float32) ** block_scale(splits[2], (NX, NY, NZ), ((0, 4), (1, 8)), -0.2, 0.2), 0.1, 0.2),
        "smoother_faces": jnp.clip(0.01 + 0.04 * jax.random.uniform(splits[3], (6, NX, NY, NZ), jnp.float32) ** block_scale(splits[3], (6, NX, NY, NZ), ((1, 4), (2, 8)), -0.2, 0.2), 0.01, 0.05),
        "send_count": draw_send_count(jax.random.fold_in(splits[17], 71), 0),
        "send_cell": draw_send_cell(jax.random.fold_in(splits[17], 71), 0),
        "restrict_col": draw_restrict_col(jax.random.fold_in(splits[17], 71), 0),
        "restrict_vals": jnp.clip(0.03 + 0.17 * jax.random.uniform(splits[7], (KR, N_GX, N_GY, NCD), jnp.float32) ** block_scale(splits[7], (KR, N_GX, N_GY, NCD), ((1, 4), (2, 8)), -0.2, 0.2), 0.03, 0.2),
        "coarse_col": draw_coarse_col(jax.random.fold_in(splits[17], 71), 0),
        "coarse_diag": jnp.clip(3.0 + 3.0 * jax.random.uniform(splits[9], (N_GX, N_GY, NCD), jnp.float32) ** block_scale(splits[9], (N_GX, N_GY, NCD), ((0, 4), (1, 8)), -0.2, 0.2), 3.0, 6.0),
        "coarse_vals": centred(splits[10], (KA, N_GX, N_GY, NCD), 0.5, 3.0, ((1, 4), (2, 8)), jnp.float32),
        "csmooth_diag": jnp.clip(0.15 + 0.15 * jax.random.uniform(splits[11], (N_GX, N_GY, NCD), jnp.float32) ** block_scale(splits[11], (N_GX, N_GY, NCD), ((0, 4), (1, 8)), -0.2, 0.2), 0.15, 0.3),
        "csmooth_vals": centred(splits[12], (KA, N_GX, N_GY, NCD), 0.05, 0.3, ((1, 4), (2, 8)), jnp.float32),
        "remote_row": draw_remote_row(jax.random.fold_in(splits[17], 71), 0),
        "remote_vals": jnp.clip(0.3 + 0.7 * jax.random.uniform(splits[14], (KI, N_GX, N_GY, 8, CAP), jnp.float32) ** block_scale(splits[14], (KI, N_GX, N_GY, 8, CAP), ((1, 4), (2, 8)), -0.2, 0.2), 0.3, 1.0),
        "interp_row": draw_interp_row(jax.random.fold_in(splits[17], 71), 0),
        "interp_vals": jnp.clip(0.3 + 0.7 * jax.random.uniform(splits[16], (KI, NX, NY, NZ), jnp.float32) ** block_scale(splits[16], (KI, NX, NY, NZ), ((1, 4), (2, 8)), -0.2, 0.2), 0.3, 1.0),
    }


OFFSETS = ((-1, -1), (-1, 0), (-1, 1), (0, -1), (0, 1), (1, -1), (1, 0), (1, 1))


def fine_neighbours(field):
    padded = jnp.pad(field, 1)
    return [padded[:-2, 1:-1, 1:-1], padded[2:, 1:-1, 1:-1],
            padded[1:-1, :-2, 1:-1], padded[1:-1, 2:, 1:-1],
            padded[1:-1, 1:-1, :-2], padded[1:-1, 1:-1, 2:]]


def apply_operator(field, diag):
    beside = fine_neighbours(field)
    beside_sum = beside[0]
    for which in range(1, 6):
        beside_sum = beside_sum + beside[which]
    return (6.0 + diag) * field - beside_sum


def apply_smoother(field, center, faces):
    beside = fine_neighbours(field)
    result = center * field
    for which in range(6):
        result = result + faces[which] * beside[which]
    return result


def to_blocks(field):
    return field.reshape(N_GX, CX, N_GY, CY, NZ).transpose(0, 2, 1, 3, 4).reshape(DEVICES, CX * CY * NZ)


def from_blocks(flat_cells):
    return flat_cells.reshape(N_GX, N_GY, CX, CY, NZ).transpose(0, 2, 1, 3, 4).reshape(NX, NY, NZ)


def lookup(table, index):
    return jax.vmap(lambda row_table, row_index: row_table[row_index], in_axes=(0, 1), out_axes=1)(table, index)


def from_neighbours(send_grid):
    padded = jnp.pad(send_grid, ((1, 1), (1, 1), (0, 0), (0, 0)))
    pieces = []
    for slot_dir in range(8):
        step_x, step_y = OFFSETS[slot_dir]
        pieces.append(padded[1 + step_x:1 + step_x + N_GX, 1 + step_y:1 + step_y + N_GY, 7 - slot_dir])
    return jnp.stack(pieces, axis=2)


def rim_of(vector):
    padded = jnp.pad(vector[:, :, :NRIM], ((1, 1), (1, 1), (0, 0)))
    pieces = []
    for slot_dir in range(8):
        step_x, step_y = OFFSETS[slot_dir]
        pieces.append(padded[1 + step_x:1 + step_x + N_GX, 1 + step_y:1 + step_y + N_GY])
    return jnp.stack(pieces, axis=2)


def coarse_apply(vector, diagonal, values, column):
    coarse_table = jnp.concatenate([vector, rim_of(vector).reshape(N_GX, N_GY, 8 * NRIM)], axis=2)
    coarse_table = coarse_table.reshape(DEVICES, NCD + 8 * NRIM)
    gathered = lookup(coarse_table, column.astype(jnp.int32).reshape(KA, DEVICES, NCD)).reshape(KA, N_GX, N_GY, NCD)
    return diagonal * vector + jnp.sum(values * gathered, axis=0)


def reference(rhs, diag, smoother_center, smoother_faces, send_count, send_cell, restrict_col,
              restrict_vals, coarse_col, coarse_diag, coarse_vals, csmooth_diag, csmooth_vals,
              remote_row, remote_vals, interp_row, interp_vals):
    cells_dev = CX * CY * NZ
    x_first = apply_smoother(rhs, smoother_center, smoother_faces)
    r_first = rhs - apply_operator(x_first, diag)
    r_blocks = to_blocks(r_first)
    cell_ids = send_cell.astype(jnp.int32).reshape(DEVICES, 8 * CAP)
    slot_ids = jnp.arange(CAP, dtype=jnp.int32)
    is_live = slot_ids[None, None, None, :] < send_count[..., None]
    picked = jnp.take_along_axis(r_blocks, cell_ids, axis=1).reshape(N_GX, N_GY, 8, CAP)
    sent_vals = jnp.where(is_live, picked, jnp.float32(0.0))
    received = from_neighbours(sent_vals).reshape(DEVICES, 8 * CAP)
    fine_table = jnp.concatenate([r_blocks, received], axis=1)
    restrict_index = restrict_col.astype(jnp.int32).reshape(KR, DEVICES, NCD)
    coarse_rhs = jnp.sum(restrict_vals.reshape(KR, DEVICES, NCD) * lookup(fine_table, restrict_index), axis=0)
    coarse_rhs = coarse_rhs.reshape(N_GX, N_GY, NCD)
    coarse_first = coarse_apply(coarse_rhs, csmooth_diag, csmooth_vals, coarse_col)
    coarse_resid = coarse_rhs - coarse_apply(coarse_first, coarse_diag, coarse_vals, coarse_col)
    coarse_second = coarse_first + coarse_apply(coarse_resid, csmooth_diag, csmooth_vals, coarse_col)
    second_flat = coarse_second.reshape(DEVICES, NCD)
    remote_index = remote_row.astype(jnp.int32).reshape(KI, DEVICES, 8 * CAP)
    back_vals = jnp.sum(remote_vals.reshape(KI, DEVICES, 8 * CAP) * lookup(second_flat, remote_index), axis=0)
    back_vals = back_vals.reshape(N_GX, N_GY, 8, CAP)
    returned = jnp.where(is_live, from_neighbours(back_vals), jnp.float32(0.0)).reshape(DEVICES, 8 * CAP)
    interp_index = jnp.stack([to_blocks(interp_row[term]) for term in range(KI)]).astype(jnp.int32)
    interp_weight = jnp.stack([to_blocks(interp_vals[term]) for term in range(KI)])
    local_part = jnp.sum(interp_weight * lookup(second_flat, interp_index), axis=0)
    scattered = jax.vmap(lambda where_to, amount: jnp.zeros((cells_dev,), jnp.float32).at[where_to].add(amount))(cell_ids, returned)
    x_second = x_first + from_blocks(local_part + scattered)
    r_second = rhs - apply_operator(x_second, diag)
    solution = x_second + apply_smoother(r_second, smoother_center, smoother_faces)
    residual = rhs - apply_operator(solution, diag)
    return solution, residual
```

```python
import jax
import jax.numpy as jnp
from jax import lax
from jax.experimental import pallas as pl
from jax.experimental.pallas import tpu as pltpu
from jax.sharding import PartitionSpec as P

BLK = 128
OFFSETS = ((-1, -1), (-1, 0), (-1, 1), (0, -1), (0, 1), (1, -1), (1, 0), (1, 1))
SIDES = ((-1, 0), (1, 0), (0, -1), (0, 1))
MESH_ID = pl.DeviceIdType.MESH


def split_two(table):
    high = table.astype(jnp.bfloat16)
    low = (table - high.astype(jnp.float32)).astype(jnp.bfloat16)
    return jnp.concatenate([high, low], axis=1)


def one_hot(base, width):
    ids = lax.broadcasted_iota(jnp.int32, (base.shape[0], width), 1)
    return jnp.where(ids == base, 1.0, 0.0).astype(jnp.bfloat16)


def pick(index, base, table_two):
    both = jnp.dot(
        one_hot(base, table_two.shape[0]), table_two, preferred_element_type=jnp.float32
    )
    rows = both[:, :BLK] + both[:, BLK:]
    return jnp.take_along_axis(rows, index & (BLK - 1), axis=1, mode="promise_in_bounds")


def make_kernel(sizes, shapes):
    na, nb = sizes
    cx, cy, nz = shapes["rhs"]
    zblocks = nz // BLK
    cells = cx * cy
    fine_rows = cells * zblocks
    cap = shapes["send_cell"][1]
    slots = cap // BLK
    kr, crows, _ = shapes["restrict_col"]
    ka = shapes["coarse_col"][0]
    ki = shapes["interp_row"][0]
    rim_rows = 8

    def fine_place(block):
        return (block % zblocks) * cells + block // zblocks

    def kernel(
        rhs_h, diag_h, center_h, faces_h, count_ref, cell_h, rcol_h, rval_h, ccol_h,
        cdiag_h, cval_h, mdiag_h, mval_h, rrow_h, rrval_h, irow_h, ival_h,
        sol_ref, res_ref,
        field, ysend, yrecv, diag, center, faces, cell, rcol, rval, ccol, cdiag, cval,
        mdiag, mval, rrow, rrval, irow, ival, resid, fine_two, choose, sent, received,
        back, returned, coarse, rim, spread,
        in_sem, halo_send, halo_recv, slot_send, slot_recv, back_send, back_recv,
        rim_send, rim_recv,
    ):
        a = lax.axis_index("gx")
        b = lax.axis_index("gy")

        loads = [
            (rhs_h, field.at[0, pl.ds(1, cx)]), (center_h, center), (faces_h, faces),
            (diag_h, diag), (cell_h, cell), (rcol_h, rcol), (rval_h, rval),
            (ccol_h, ccol), (mdiag_h, mdiag), (mval_h, mval), (cdiag_h, cdiag),
            (cval_h, cval), (rrow_h, rrow), (rrval_h, rrval), (irow_h, irow),
            (ival_h, ival),
        ]
        loads = [
            pltpu.make_async_copy(source, target, in_sem.at[n])
            for n, (source, target) in enumerate(loads)
        ]
        for load in loads:
            load.start()

        def there(step):
            dx, dy = step
            checks = []
            if dx < 0:
                checks.append(a > 0)
            if dx > 0:
                checks.append(a < na - 1)
            if dy < 0:
                checks.append(b > 0)
            if dy > 0:
                checks.append(b < nb - 1)
            out = checks[0]
            for check in checks[1:]:
                out = jnp.logical_and(out, check)
            return out

        exists = [there(step) for step in OFFSETS]
        side_exists = [there(step) for step in SIDES]

        barrier = pltpu.get_barrier_semaphore()
        total = jnp.int32(0)
        for d, (dx, dy) in enumerate(OFFSETS):
            @pl.when(exists[d])
            def _():
                pl.semaphore_signal(
                    barrier, inc=1, device_id=(a + dx, b + dy), device_id_type=MESH_ID
                )
            total = total + exists[d].astype(jnp.int32)

        for s in range(4):
            @pl.when(jnp.logical_not(side_exists[s]))
            def _():
                for t in range(5):
                    if s < 2:
                        field[t, 0 if s == 0 else cx + 1] = jnp.zeros((cy, nz), jnp.float32)
                    else:
                        yrecv[t, s - 2] = jnp.zeros((cx, nz), jnp.float32)
        for d in range(8):
            @pl.when(jnp.logical_not(exists[d]))
            def _():
                received[d] = jnp.zeros((slots, BLK), jnp.float32)
                returned[d] = jnp.zeros((slots, BLK), jnp.float32)
                for t in range(3):
                    rim[t, d] = jnp.zeros((rim_rows, BLK), jnp.float32)

        def halo_copy(t, s):
            dx, dy = SIDES[s]
            if s == 0:
                src, dst = field.at[t, 1], field.at[t, cx + 1]
            elif s == 1:
                src, dst = field.at[t, cx], field.at[t, 0]
            else:
                src, dst = ysend.at[t, s - 2], yrecv.at[t, 3 - s]
            return pltpu.make_async_remote_copy(
                src_ref=src, dst_ref=dst, send_sem=halo_send.at[t, s],
                recv_sem=halo_recv.at[t, s ^ 1],
                device_id=(a + dx, b + dy), device_id_type=MESH_ID,
            )

        def halo_arrival(t, s):
            dx, dy = SIDES[s]
            dst = field.at[t, 0 if s == 0 else cx + 1] if s < 2 else yrecv.at[t, s - 2]
            return pltpu.make_async_remote_copy(
                src_ref=dst, dst_ref=dst, send_sem=halo_send.at[t, s],
                recv_sem=halo_recv.at[t, s],
                device_id=(a + dx, b + dy), device_id_type=MESH_ID,
            )

        def start_halo(t):
            for s in range(4):
                @pl.when(side_exists[s])
                def _():
                    halo_copy(t, s).start()

        def wait_halo(t):
            for s in range(4):
                @pl.when(side_exists[s])
                def _():
                    halo_arrival(t, s).wait_recv()

        def eight_copy(src, dst, send_sem, recv_sem, d):
            dx, dy = OFFSETS[d]
            return pltpu.make_async_remote_copy(
                src_ref=src(d), dst_ref=dst(7 - d), send_sem=send_sem(d),
                recv_sem=recv_sem(7 - d),
                device_id=(a + dx, b + dy), device_id_type=MESH_ID,
            )

        def eight_arrival(dst, send_sem, recv_sem, d):
            dx, dy = OFFSETS[d]
            return pltpu.make_async_remote_copy(
                src_ref=dst(d), dst_ref=dst(d), send_sem=send_sem(d), recv_sem=recv_sem(d),
                device_id=(a + dx, b + dy), device_id_type=MESH_ID,
            )

        slot_plan = (
            lambda d: sent.at[d], lambda d: received.at[d],
            lambda d: slot_send.at[d], lambda d: slot_recv.at[d],
        )
        back_plan = (
            lambda d: back.at[d], lambda d: returned.at[d],
            lambda d: back_send.at[d], lambda d: back_recv.at[d],
        )

        def rim_plan(t):
            return (
                lambda d: coarse.at[t, pl.ds(0, rim_rows)], lambda d: rim.at[t, d],
                lambda d: rim_send.at[t, d], lambda d: rim_recv.at[t, d],
            )

        def start_eight(plan):
            for d in range(8):
                @pl.when(exists[d])
                def _():
                    eight_copy(*plan, d).start()

        def wait_eight(plan):
            for d in range(8):
                @pl.when(exists[d])
                def _():
                    eight_arrival(*plan[1:], d).wait_recv()

        row_ids = lax.broadcasted_iota(jnp.int32, (cy, nz), 0)
        lane_ids = lax.broadcasted_iota(jnp.int32, (cy, nz), 1)

        def beside(t, i):
            centre = field[t, i + 1]
            low = jnp.broadcast_to(yrecv[t, 0, i:i + 1, :], (cy, nz))
            high = jnp.broadcast_to(yrecv[t, 1, i:i + 1, :], (cy, nz))
            return centre, [
                field[t, i],
                field[t, i + 2],
                jnp.where(row_ids == 0, low, pltpu.roll(centre, 1, 0)),
                jnp.where(row_ids == cy - 1, high, pltpu.roll(centre, cy - 1, 0)),
                jnp.where(lane_ids == 0, 0.0, pltpu.roll(centre, 1, 1)),
                jnp.where(lane_ids == nz - 1, 0.0, pltpu.roll(centre, nz - 1, 1)),
            ]

        def operator(t, i):
            centre, near = beside(t, i)
            sums = near[0]
            for one in near[1:]:
                sums = sums + one
            return (6.0 + diag[i]) * centre - sums

        def smoother(t, i):
            centre, near = beside(t, i)
            out = center[i] * centre
            for q in range(6):
                out = out + faces[q, i] * near[q]
            return out

        def put(t, i, value):
            field[t, i + 1] = value
            ysend[t, 0, i:i + 1, :] = value[0:1]
            ysend[t, 1, i:i + 1, :] = value[cy - 1:cy]

        loads[0].wait()
        for i in range(cx):
            value = field[0, i + 1]
            ysend[0, 0, i:i + 1, :] = value[0:1]
            ysend[0, 1, i:i + 1, :] = value[cy - 1:cy]
        pl.semaphore_wait(barrier, total)
        start_halo(0)
        for load in loads[1:5]:
            load.wait()

        cell_index = jnp.concatenate(
            [cell[:, s * BLK:(s + 1) * BLK] for s in range(slots)], axis=0
        )
        cell_base = fine_place(cell_index[:, 0:1] // BLK)
        across = jnp.transpose(
            jnp.broadcast_to(cell_base, (8 * slots, BLK)).astype(jnp.float32)
        )[0:1].astype(jnp.int32)
        fine_ids = lax.broadcasted_iota(jnp.int32, (fine_rows, 8 * slots), 0)
        choose[...] = jnp.where(fine_ids == across, 1.0, 0.0).astype(jnp.bfloat16)

        wait_halo(0)
        for i in range(cx):
            put(1, i, smoother(0, i))
        start_halo(1)
        for load in loads[5:]:
            load.wait()

        wait_halo(1)
        for i in range(cx):
            resid[i] = field[0, i + 1] - operator(1, i)
        table = jnp.concatenate(
            [resid[:, :, z * BLK:(z + 1) * BLK].reshape(cells, BLK) for z in range(zblocks)],
            axis=0,
        )
        fine_two[...] = split_two(table)

        picked = pick(cell_index, cell_base, fine_two[...])
        lanes = lax.broadcasted_iota(jnp.int32, (8, BLK), 1)
        for s in range(slots):
            live = lanes + s * BLK < count_ref[...]
            values = jnp.where(live, picked[8 * s:8 * s + 8], 0.0)
            for d in range(8):
                sent[d, s:s + 1, :] = values[d:d + 1]
        start_eight(slot_plan)

        step = 9 if kr % 9 == 0 else 1

        def restrict_some(c, acc):
            index = rcol[pl.ds(c * step, step)].reshape(step * crows, BLK)
            block = index[:, 0:1] // BLK
            base = jnp.where(block < fine_rows, fine_place(block), -1)
            got = pick(index, base, fine_two[...]).reshape(step, crows, BLK)
            return acc + jnp.sum(got * rval[pl.ds(c * step, step)], axis=0)

        rc = lax.fori_loop(
            0, kr // step, restrict_some, jnp.zeros((crows, BLK), jnp.float32)
        )
        wait_eight(slot_plan)
        received_two = split_two(received[...].reshape(8 * slots, BLK))
        index = rcol[:, 0:rim_rows, :].reshape(kr * rim_rows, BLK)
        got = pick(index, index[:, 0:1] // BLK - fine_rows, received_two)
        more = jnp.sum(
            got.reshape(kr, rim_rows, BLK) * rval[:, 0:rim_rows, :], axis=0
        )
        rc = jnp.concatenate([rc[:rim_rows] + more, rc[rim_rows:]], axis=0)

        def coarse_apply(t, vector, diagonal, values):
            coarse[t] = vector
            start_eight(rim_plan(t))
            index = ccol[...].reshape(ka * crows, BLK)
            got = pick(index, index[:, 0:1] // BLK, split_two(vector))
            own = diagonal[...] * vector + jnp.sum(
                got.reshape(ka, crows, BLK) * values[...], axis=0
            )
            wait_eight(rim_plan(t))
            index = ccol[:, 0:rim_rows, :].reshape(ka * rim_rows, BLK)
            got = pick(
                index, index[:, 0:1] // BLK - crows,
                split_two(rim[t].reshape(8 * rim_rows, BLK)),
            )
            more = jnp.sum(
                got.reshape(ka, rim_rows, BLK) * values[:, 0:rim_rows, :], axis=0
            )
            return jnp.concatenate([own[:rim_rows] + more, own[rim_rows:]], axis=0)

        xc1 = coarse_apply(0, rc, mdiag, mval)
        rc2 = rc - coarse_apply(1, xc1, cdiag, cval)
        xc2 = xc1 + coarse_apply(2, rc2, mdiag, mval)
        coarse_two = split_two(xc2)

        group = 8 if slots % 8 == 0 else 1
        for c in range(slots // group):
            parts = [(c * group + g) * BLK for g in range(group)]
            index = jnp.concatenate(
                [rrow[:, :, p:p + BLK].reshape(ki * 8, BLK) for p in parts], axis=0
            )
            got = pick(index, index[:, 0:1] // BLK, coarse_two)
            for g, p in enumerate(parts):
                mine = got[g * ki * 8:(g + 1) * ki * 8].reshape(ki, 8, BLK)
                values = jnp.sum(mine * rrval[:, :, p:p + BLK], axis=0)
                for d in range(8):
                    back[d, c * group + g:c * group + g + 1, :] = values[d:d + 1]
        start_eight(back_plan)

        for z in range(zblocks):
            p = z * BLK
            index = irow[:, :, :, p:p + BLK].reshape(ki * cells, BLK)
            got = pick(index, index[:, 0:1] // BLK, coarse_two)
            got = got.reshape(ki, cx, cy, BLK) * ival[:, :, :, p:p + BLK]
            field[2, 1:cx + 1, :, p:p + BLK] = (
                field[1, 1:cx + 1, :, p:p + BLK] + jnp.sum(got, axis=0)
            )
        wait_eight(back_plan)

        lane_of = lax.broadcasted_iota(jnp.int32, (BLK, BLK), 0)
        pair_row = lax.broadcasted_iota(jnp.int32, (16, BLK), 0) % 8

        def spread_some(s, carry):
            p = pl.multiple_of(s * BLK, BLK)
            values = jnp.concatenate(
                [returned[d, pl.ds(s, 1), :] for d in range(8)], axis=0
            )
            values = jnp.where(lanes + p < count_ref[...], values, 0.0)
            high = values.astype(jnp.bfloat16)
            low = (values - high.astype(jnp.float32)).astype(jnp.bfloat16)
            pair = jnp.concatenate([high, low], axis=0)
            acc = jnp.zeros((16, BLK), jnp.float32)
            for d in range(8):
                within = cell[d:d + 1, pl.ds(p, BLK)] & (BLK - 1)
                place = jnp.where(lane_of == within, 1.0, 0.0).astype(jnp.bfloat16)
                one = lax.dot_general(
                    pair, place, (((1,), (1,)), ((), ())),
                    preferred_element_type=jnp.float32,
                )
                acc = jnp.where(pair_row == d, one, acc)
            spread[pl.ds(pl.multiple_of(s * 8, 8), 8)] = acc[0:8] + acc[8:16]
            return carry

        lax.fori_loop(0, slots, spread_some, 0)
        both = jnp.dot(
            choose[...], split_two(spread[...]), preferred_element_type=jnp.float32
        )
        added = both[:, :BLK] + both[:, BLK:]
        for z in range(zblocks):
            p = z * BLK
            field[2, 1:cx + 1, :, p:p + BLK] = (
                field[2, 1:cx + 1, :, p:p + BLK]
                + added[z * cells:(z + 1) * cells].reshape(cx, cy, BLK)
            )
        for i in range(cx):
            value = field[2, i + 1]
            ysend[2, 0, i:i + 1, :] = value[0:1]
            ysend[2, 1, i:i + 1, :] = value[cy - 1:cy]
        start_halo(2)
        wait_halo(2)

        for i in range(cx):
            put(3, i, field[0, i + 1] - operator(2, i))
        start_halo(3)
        wait_halo(3)
        for i in range(cx):
            value = field[2, i + 1] + smoother(3, i)
            put(4, i, value)
            sol_ref[i] = value
        start_halo(4)
        wait_halo(4)
        for i in range(cx):
            res_ref[i] = field[0, i + 1] - operator(4, i)

        for t in range(5):
            for s in range(4):
                @pl.when(side_exists[s])
                def _():
                    halo_copy(t, s).wait_send()
        for plan in (slot_plan, back_plan, rim_plan(0), rim_plan(1), rim_plan(2)):
            for d in range(8):
                @pl.when(exists[d])
                def _():
                    eight_copy(*plan, d).wait_send()

    f32, i32, bf16 = jnp.float32, jnp.int32, jnp.bfloat16
    vm = pltpu.VMEM
    dma = pltpu.SemaphoreType.DMA
    scratch = [
        vm((5, cx + 2, cy, nz), f32), vm((5, 2, cx, nz), f32), vm((5, 2, cx, nz), f32),
        vm((cx, cy, nz), f32), vm((cx, cy, nz), f32), vm((6, cx, cy, nz), f32),
        vm((8, cap), i32), vm((kr, crows, BLK), i32), vm((kr, crows, BLK), f32),
        vm((ka, crows, BLK), i32), vm((crows, BLK), f32), vm((ka, crows, BLK), f32),
        vm((crows, BLK), f32), vm((ka, crows, BLK), f32),
        vm((ki, 8, cap), i32), vm((ki, 8, cap), f32),
        vm((ki, cx, cy, nz), i32), vm((ki, cx, cy, nz), f32),
        vm((cx, cy, nz), f32), vm((fine_rows, 2 * BLK), bf16),
        vm((fine_rows, 8 * slots), bf16),
        vm((8, slots, BLK), f32), vm((8, slots, BLK), f32),
        vm((8, slots, BLK), f32), vm((8, slots, BLK), f32),
        vm((3, crows, BLK), f32), vm((3, 8, rim_rows, BLK), f32),
        vm((8 * slots, BLK), f32),
        dma((16,)), dma((5, 4)), dma((5, 4)), dma((8,)), dma((8,)), dma((8,)), dma((8,)),
        dma((3, 8)), dma((3, 8)),
    ]
    whole = pl.BlockSpec(memory_space=pltpu.VMEM)
    anywhere = pl.BlockSpec(memory_space=pl.ANY)
    return pl.pallas_call(
        kernel,
        out_shape=(
            jax.ShapeDtypeStruct((cx, cy, nz), f32),
            jax.ShapeDtypeStruct((cx, cy, nz), f32),
        ),
        in_specs=[anywhere] * 4 + [whole] + [anywhere] * 12,
        out_specs=(whole, whole),
        scratch_shapes=scratch,
        compiler_params=pltpu.CompilerParams(
            collective_id=0, has_side_effects=True, vmem_limit_bytes=40 * 1024 * 1024
        ),
        name="vcycle",
    )


def body(
    rhs, diag, smoother_center, smoother_faces, send_count, send_cell, restrict_col,
    restrict_vals, coarse_col, coarse_diag, coarse_vals, csmooth_diag, csmooth_vals,
    remote_row, remote_vals, interp_row, interp_vals,
):
    def rows(array):
        return array.reshape(array.shape[0], -1, BLK)

    cap = send_cell.shape[-1]
    ki = remote_row.shape[0]
    operands = (
        rhs, diag, smoother_center, smoother_faces,
        jnp.broadcast_to(send_count.reshape(8, 1), (8, BLK)),
        send_cell.reshape(8, cap), rows(restrict_col), rows(restrict_vals),
        rows(coarse_col), coarse_diag.reshape(-1, BLK), rows(coarse_vals),
        csmooth_diag.reshape(-1, BLK), rows(csmooth_vals),
        remote_row.reshape(ki, 8, cap), remote_vals.reshape(ki, 8, cap),
        interp_row, interp_vals,
    )
    shapes = {
        "rhs": rhs.shape, "send_cell": (8, cap), "restrict_col": operands[6].shape,
        "coarse_col": operands[8].shape, "interp_row": interp_row.shape,
    }
    sizes = (lax.axis_size("gx"), lax.axis_size("gy"))
    return make_kernel(sizes, shapes)(*operands)


def solution(mesh):
    fine = P("gx", "gy", None)
    listed = P(None, "gx", "gy", None)
    placed = (
        fine, fine, fine, listed, fine, P("gx", "gy", None, None), listed, listed,
        listed, fine, listed, fine, listed,
        P(None, "gx", "gy", None, None), P(None, "gx", "gy", None, None),
        listed, listed,
    )
    return jax.shard_map(
        body, mesh=mesh, in_specs=placed, out_specs=(fine, fine), check_vma=False
    )
```

```python
import jax
import jax.numpy as jnp
from jax import lax
from jax.experimental import pallas as pl
from jax.experimental.pallas import tpu as pltpu
from jax.sharding import PartitionSpec as P

BLK = 128
OFFSETS = ((-1, -1), (-1, 0), (-1, 1), (0, -1), (0, 1), (1, -1), (1, 0), (1, 1))
SIDES = ((-1, 0), (1, 0), (0, -1), (0, 1))
MESH_ID = pl.DeviceIdType.MESH


def split_two(table):
    high = table.astype(jnp.bfloat16)
    low = (table - high.astype(jnp.float32)).astype(jnp.bfloat16)
    return jnp.concatenate([high, low], axis=1)


def one_hot(base, width):
    ids = lax.broadcasted_iota(jnp.int32, (base.shape[0], width), 1)
    return jnp.where(ids == base, 1.0, 0.0).astype(jnp.bfloat16)


def pick(index, base, table_two):
    both = jnp.dot(
        one_hot(base, table_two.shape[0]), table_two, preferred_element_type=jnp.float32
    )
    rows = both[:, :BLK] + both[:, BLK:]
    return jnp.take_along_axis(rows, index & (BLK - 1), axis=1, mode="promise_in_bounds")


def make_kernel(sizes, shapes):
    na, nb = sizes
    cx, cy, nz = shapes["rhs"]
    zblocks = nz // BLK
    cells = cx * cy
    fine_rows = cells * zblocks
    cap = shapes["send_cell"][1]
    slots = cap // BLK
    kr, crows, _ = shapes["restrict_col"]
    ka = shapes["coarse_col"][0]
    ki = shapes["interp_row"][0]
    rim_rows = 8

    def fine_place(block):
        return (block % zblocks) * cells + block // zblocks

    def kernel(
        rhs_h, diag_h, center_h, faces_h, count_ref, cell_h, rcol_h, rval_h, ccol_h,
        cdiag_h, cval_h, mdiag_h, mval_h, rrow_h, rrval_h, irow_h, ival_h,
        sol_ref, res_ref,
        field, ysend, yrecv, diag, center, faces, cell, rcol, rval, ccol, cdiag, cval,
        mdiag, mval, rrow, rrval, irow, ival, resid, fine_two, choose, sent, received,
        back, returned, coarse, rim, spread,
        in_sem, halo_send, halo_recv, slot_send, slot_recv, back_send, back_recv,
        rim_send, rim_recv,
    ):
        a = lax.axis_index("gx")
        b = lax.axis_index("gy")

        loads = [
            (rhs_h, field.at[0, pl.ds(1, cx)]), (center_h, center), (faces_h, faces),
            (diag_h, diag), (cell_h, cell), (rcol_h, rcol), (rval_h, rval),
            (ccol_h, ccol), (mdiag_h, mdiag), (mval_h, mval), (cdiag_h, cdiag),
            (cval_h, cval), (rrow_h, rrow), (rrval_h, rrval), (irow_h, irow),
            (ival_h, ival),
        ]
        loads = [
            pltpu.make_async_copy(source, target, in_sem.at[n])
            for n, (source, target) in enumerate(loads)
        ]
        for load in loads:
            load.start()

        def there(step):
            dx, dy = step
            checks = []
            if dx < 0:
                checks.append(a > 0)
            if dx > 0:
                checks.append(a < na - 1)
            if dy < 0:
                checks.append(b > 0)
            if dy > 0:
                checks.append(b < nb - 1)
            out = checks[0]
            for check in checks[1:]:
                out = jnp.logical_and(out, check)
            return out

        exists = [there(step) for step in OFFSETS]
        side_exists = [there(step) for step in SIDES]

        barrier = pltpu.get_barrier_semaphore()
        total = jnp.int32(0)
        for d, (dx, dy) in enumerate(OFFSETS):
            @pl.when(exists[d])
            def _():
                pl.semaphore_signal(
                    barrier, inc=1, device_id=(a + dx, b + dy), device_id_type=MESH_ID
                )
            total = total + exists[d].astype(jnp.int32)

        for s in range(4):
            @pl.when(jnp.logical_not(side_exists[s]))
            def _():
                for t in range(5):
                    if s < 2:
                        field[t, 0 if s == 0 else cx + 1] = jnp.zeros((cy, nz), jnp.float32)
                    else:
                        yrecv[t, s - 2] = jnp.zeros((cx, nz), jnp.float32)
        for d in range(8):
            @pl.when(jnp.logical_not(exists[d]))
            def _():
                received[d] = jnp.zeros((slots, BLK), jnp.float32)
                returned[d] = jnp.zeros((slots, BLK), jnp.float32)
                for t in range(3):
                    rim[t, d] = jnp.zeros((rim_rows, BLK), jnp.float32)

        def halo_copy(t, s):
            dx, dy = SIDES[s]
            if s == 0:
                src, dst = field.at[t, 1], field.at[t, cx + 1]
            elif s == 1:
                src, dst = field.at[t, cx], field.at[t, 0]
            else:
                src, dst = ysend.at[t, s - 2], yrecv.at[t, 3 - s]
            return pltpu.make_async_remote_copy(
                src_ref=src, dst_ref=dst, send_sem=halo_send.at[t, s],
                recv_sem=halo_recv.at[t, s ^ 1],
                device_id=(a + dx, b + dy), device_id_type=MESH_ID,
            )

        def halo_arrival(t, s):
            dx, dy = SIDES[s]
            dst = field.at[t, 0 if s == 0 else cx + 1] if s < 2 else yrecv.at[t, s - 2]
            return pltpu.make_async_remote_copy(
                src_ref=dst, dst_ref=dst, send_sem=halo_send.at[t, s],
                recv_sem=halo_recv.at[t, s],
                device_id=(a + dx, b + dy), device_id_type=MESH_ID,
            )

        def start_halo(t):
            for s in range(4):
                @pl.when(side_exists[s])
                def _():
                    halo_copy(t, s).start()

        def wait_halo(t):
            for s in range(4):
                @pl.when(side_exists[s])
                def _():
                    halo_arrival(t, s).wait_recv()

        def eight_copy(src, dst, send_sem, recv_sem, d):
            dx, dy = OFFSETS[d]
            return pltpu.make_async_remote_copy(
                src_ref=src(d), dst_ref=dst(7 - d), send_sem=send_sem(d),
                recv_sem=recv_sem(7 - d),
                device_id=(a + dx, b + dy), device_id_type=MESH_ID,
            )

        def eight_arrival(dst, send_sem, recv_sem, d):
            dx, dy = OFFSETS[d]
            return pltpu.make_async_remote_copy(
                src_ref=dst(d), dst_ref=dst(d), send_sem=send_sem(d), recv_sem=recv_sem(d),
                device_id=(a + dx, b + dy), device_id_type=MESH_ID,
            )

        slot_plan = (
            lambda d: sent.at[d], lambda d: received.at[d],
            lambda d: slot_send.at[d], lambda d: slot_recv.at[d],
        )
        back_plan = (
            lambda d: back.at[d], lambda d: returned.at[d],
            lambda d: back_send.at[d], lambda d: back_recv.at[d],
        )

        def rim_plan(t):
            return (
                lambda d: coarse.at[t, pl.ds(0, rim_rows)], lambda d: rim.at[t, d],
                lambda d: rim_send.at[t, d], lambda d: rim_recv.at[t, d],
            )

        def start_eight(plan):
            for d in range(8):
                @pl.when(exists[d])
                def _():
                    eight_copy(*plan, d).start()

        def wait_eight(plan):
            for d in range(8):
                @pl.when(exists[d])
                def _():
                    eight_arrival(*plan[1:], d).wait_recv()

        row_ids = lax.broadcasted_iota(jnp.int32, (cy, nz), 0)
        lane_ids = lax.broadcasted_iota(jnp.int32, (cy, nz), 1)

        def beside(t, i):
            centre = field[t, i + 1]
            low = jnp.broadcast_to(yrecv[t, 0, i:i + 1, :], (cy, nz))
            high = jnp.broadcast_to(yrecv[t, 1, i:i + 1, :], (cy, nz))
            return centre, [
                field[t, i],
                field[t, i + 2],
                jnp.where(row_ids == 0, low, pltpu.roll(centre, 1, 0)),
                jnp.where(row_ids == cy - 1, high, pltpu.roll(centre, cy - 1, 0)),
                jnp.where(lane_ids == 0, 0.0, pltpu.roll(centre, 1, 1)),
                jnp.where(lane_ids == nz - 1, 0.0, pltpu.roll(centre, nz - 1, 1)),
            ]

        def operator(t, i):
            centre, near = beside(t, i)
            sums = near[0]
            for one in near[1:]:
                sums = sums + one
            return (6.0 + diag[i]) * centre - sums

        def smoother(t, i):
            centre, near = beside(t, i)
            out = center[i] * centre
            for q in range(6):
                out = out + faces[q, i] * near[q]
            return out

        def put(t, i, value):
            field[t, i + 1] = value
            ysend[t, 0, i:i + 1, :] = value[0:1]
            ysend[t, 1, i:i + 1, :] = value[cy - 1:cy]

        loads[0].wait()
        for i in range(cx):
            value = field[0, i + 1]
            ysend[0, 0, i:i + 1, :] = value[0:1]
            ysend[0, 1, i:i + 1, :] = value[cy - 1:cy]
        pl.semaphore_wait(barrier, total)
        start_halo(0)
        for load in loads[1:5]:
            load.wait()

        cell_index = jnp.concatenate(
            [cell[:, s * BLK:(s + 1) * BLK] for s in range(slots)], axis=0
        )
        cell_base = fine_place(cell_index[:, 0:1] // BLK)
        across = jnp.transpose(
            jnp.broadcast_to(cell_base, (8 * slots, BLK)).astype(jnp.float32)
        )[0:1].astype(jnp.int32)
        fine_ids = lax.broadcasted_iota(jnp.int32, (fine_rows, 8 * slots), 0)
        choose[...] = jnp.where(fine_ids == across, 1.0, 0.0).astype(jnp.bfloat16)

        wait_halo(0)
        for i in range(cx):
            put(1, i, smoother(0, i))
        start_halo(1)
        for load in loads[5:]:
            load.wait()

        wait_halo(1)
        for i in range(cx):
            resid[i] = field[0, i + 1] - operator(1, i)
        table = jnp.concatenate(
            [resid[:, :, z * BLK:(z + 1) * BLK].reshape(cells, BLK) for z in range(zblocks)],
            axis=0,
        )
        fine_two[...] = split_two(table)

        picked = pick(cell_index, cell_base, fine_two[...])
        lanes = lax.broadcasted_iota(jnp.int32, (8, BLK), 1)
        for s in range(slots):
            live = lanes + s * BLK < count_ref[...]
            values = jnp.where(live, picked[8 * s:8 * s + 8], 0.0)
            for d in range(8):
                sent[d, s:s + 1, :] = values[d:d + 1]
        start_eight(slot_plan)

        step = 9 if kr % 9 == 0 else 1

        def restrict_some(c, acc):
            index = rcol[pl.ds(c * step, step)].reshape(step * crows, BLK)
            block = index[:, 0:1] // BLK
            base = jnp.where(block < fine_rows, fine_place(block), -1)
            got = pick(index, base, fine_two[...]).reshape(step, crows, BLK)
            return acc + jnp.sum(got * rval[pl.ds(c * step, step)], axis=0)

        rc = lax.fori_loop(
            0, kr // step, restrict_some, jnp.zeros((crows, BLK), jnp.float32)
        )
        wait_eight(slot_plan)
        received_two = split_two(received[...].reshape(8 * slots, BLK))
        index = rcol[:, 0:rim_rows, :].reshape(kr * rim_rows, BLK)
        got = pick(index, index[:, 0:1] // BLK - fine_rows, received_two)
        more = jnp.sum(
            got.reshape(kr, rim_rows, BLK) * rval[:, 0:rim_rows, :], axis=0
        )
        rc = jnp.concatenate([rc[:rim_rows] + more, rc[rim_rows:]], axis=0)

        def coarse_apply(t, vector, diagonal, values):
            coarse[t] = vector
            start_eight(rim_plan(t))
            index = ccol[...].reshape(ka * crows, BLK)
            got = pick(index, index[:, 0:1] // BLK, split_two(vector))
            own = diagonal[...] * vector + jnp.sum(
                got.reshape(ka, crows, BLK) * values[...], axis=0
            )
            wait_eight(rim_plan(t))
            index = ccol[:, 0:rim_rows, :].reshape(ka * rim_rows, BLK)
            got = pick(
                index, index[:, 0:1] // BLK - crows,
                split_two(rim[t].reshape(8 * rim_rows, BLK)),
            )
            more = jnp.sum(
                got.reshape(ka, rim_rows, BLK) * values[:, 0:rim_rows, :], axis=0
            )
            return jnp.concatenate([own[:rim_rows] + more, own[rim_rows:]], axis=0)

        xc1 = coarse_apply(0, rc, mdiag, mval)
        rc2 = rc - coarse_apply(1, xc1, cdiag, cval)
        xc2 = xc1 + coarse_apply(2, rc2, mdiag, mval)
        coarse_two = split_two(xc2)

        group = 8 if slots % 8 == 0 else 1
        for c in range(slots // group):
            parts = [(c * group + g) * BLK for g in range(group)]
            index = jnp.concatenate(
                [rrow[:, :, p:p + BLK].reshape(ki * 8, BLK) for p in parts], axis=0
            )
            got = pick(index, index[:, 0:1] // BLK, coarse_two)
            for g, p in enumerate(parts):
                mine = got[g * ki * 8:(g + 1) * ki * 8].reshape(ki, 8, BLK)
                values = jnp.sum(mine * rrval[:, :, p:p + BLK], axis=0)
                for d in range(8):
                    back[d, c * group + g:c * group + g + 1, :] = values[d:d + 1]
        start_eight(back_plan)

        for z in range(zblocks):
            p = z * BLK
            index = irow[:, :, :, p:p + BLK].reshape(ki * cells, BLK)
            got = pick(index, index[:, 0:1] // BLK, coarse_two)
            got = got.reshape(ki, cx, cy, BLK) * ival[:, :, :, p:p + BLK]
            field[2, 1:cx + 1, :, p:p + BLK] = (
                field[1, 1:cx + 1, :, p:p + BLK] + jnp.sum(got, axis=0)
            )
        wait_eight(back_plan)

        fold_rows = lax.broadcasted_iota(jnp.int32, (64, BLK), 0)
        fold_lanes = lax.broadcasted_iota(jnp.int32, (64, BLK), 1)
        fold_index = (fold_lanes % 16) * 8 + fold_rows % 8
        fold_keep = fold_lanes // 16 == fold_rows // 8

        def spread_some(s, carry):
            p = pl.multiple_of(s * BLK, BLK)
            values = jnp.concatenate(
                [returned[d, pl.ds(s, 1), :] for d in range(8)], axis=0
            )
            values = jnp.where(lanes + p < count_ref[...], values, 0.0)
            within = cell[:, pl.ds(p, BLK)] & (BLK - 1)
            upper, lower = within // 16, within % 16
            coarse_part = jnp.concatenate(
                [jnp.where(upper == h, values, 0.0) for h in range(8)], axis=0
            )
            high = coarse_part.astype(jnp.bfloat16)
            low = (coarse_part - high.astype(jnp.float32)).astype(jnp.bfloat16)
            fine_part = jnp.concatenate(
                [jnp.where(lower == l, 1.0, 0.0) for l in range(16)], axis=0
            ).astype(jnp.bfloat16)
            out = lax.dot_general(
                jnp.concatenate([high, low], axis=0), fine_part,
                (((1,), (1,)), ((), ())), preferred_element_type=jnp.float32,
            )
            out = jnp.take_along_axis(
                out[:64] + out[64:], fold_index, axis=1, mode="promise_in_bounds"
            )
            out = jnp.where(fold_keep, out, 0.0).reshape(8, 8, BLK)
            spread[pl.ds(pl.multiple_of(s * 8, 8), 8)] = jnp.sum(out, axis=0)
            return carry

        lax.fori_loop(0, slots, spread_some, 0, unroll=32)
        both = jnp.dot(
            choose[...], split_two(spread[...]), preferred_element_type=jnp.float32
        )
        added = both[:, :BLK] + both[:, BLK:]
        for z in range(zblocks):
            p = z * BLK
            field[2, 1:cx + 1, :, p:p + BLK] = (
                field[2, 1:cx + 1, :, p:p + BLK]
                + added[z * cells:(z + 1) * cells].reshape(cx, cy, BLK)
            )
        for i in range(cx):
            value = field[2, i + 1]
            ysend[2, 0, i:i + 1, :] = value[0:1]
            ysend[2, 1, i:i + 1, :] = value[cy - 1:cy]
        start_halo(2)
        wait_halo(2)

        for i in range(cx):
            put(3, i, field[0, i + 1] - operator(2, i))
        start_halo(3)
        wait_halo(3)
        for i in range(cx):
            value = field[2, i + 1] + smoother(3, i)
            put(4, i, value)
            sol_ref[i] = value
        start_halo(4)
        wait_halo(4)
        for i in range(cx):
            res_ref[i] = field[0, i + 1] - operator(4, i)

        for t in range(5):
            for s in range(4):
                @pl.when(side_exists[s])
                def _():
                    halo_copy(t, s).wait_send()
        for plan in (slot_plan, back_plan, rim_plan(0), rim_plan(1), rim_plan(2)):
            for d in range(8):
                @pl.when(exists[d])
                def _():
                    eight_copy(*plan, d).wait_send()

    f32, i32, bf16 = jnp.float32, jnp.int32, jnp.bfloat16
    vm = pltpu.VMEM
    dma = pltpu.SemaphoreType.DMA
    scratch = [
        vm((5, cx + 2, cy, nz), f32), vm((5, 2, cx, nz), f32), vm((5, 2, cx, nz), f32),
        vm((cx, cy, nz), f32), vm((cx, cy, nz), f32), vm((6, cx, cy, nz), f32),
        vm((8, cap), i32), vm((kr, crows, BLK), i32), vm((kr, crows, BLK), f32),
        vm((ka, crows, BLK), i32), vm((crows, BLK), f32), vm((ka, crows, BLK), f32),
        vm((crows, BLK), f32), vm((ka, crows, BLK), f32),
        vm((ki, 8, cap), i32), vm((ki, 8, cap), f32),
        vm((ki, cx, cy, nz), i32), vm((ki, cx, cy, nz), f32),
        vm((cx, cy, nz), f32), vm((fine_rows, 2 * BLK), bf16),
        vm((fine_rows, 8 * slots), bf16),
        vm((8, slots, BLK), f32), vm((8, slots, BLK), f32),
        vm((8, slots, BLK), f32), vm((8, slots, BLK), f32),
        vm((3, crows, BLK), f32), vm((3, 8, rim_rows, BLK), f32),
        vm((8 * slots, BLK), f32),
        dma((16,)), dma((5, 4)), dma((5, 4)), dma((8,)), dma((8,)), dma((8,)), dma((8,)),
        dma((3, 8)), dma((3, 8)),
    ]
    whole = pl.BlockSpec(memory_space=pltpu.VMEM)
    in_hbm = pl.BlockSpec(memory_space=pltpu.HBM)
    return pl.pallas_call(
        kernel,
        out_shape=(
            jax.ShapeDtypeStruct((cx, cy, nz), f32),
            jax.ShapeDtypeStruct((cx, cy, nz), f32),
        ),
        in_specs=[in_hbm] * 4 + [whole] + [in_hbm] * 12,
        out_specs=(whole, whole),
        scratch_shapes=scratch,
        compiler_params=pltpu.CompilerParams(
            collective_id=0, has_side_effects=True, vmem_limit_bytes=40 * 1024 * 1024
        ),
        name="vcycle",
    )


def body(
    rhs, diag, smoother_center, smoother_faces, send_count, send_cell, restrict_col,
    restrict_vals, coarse_col, coarse_diag, coarse_vals, csmooth_diag, csmooth_vals,
    remote_row, remote_vals, interp_row, interp_vals,
):
    def rows(array):
        return array.reshape(array.shape[0], -1, BLK)

    cap = send_cell.shape[-1]
    ki = remote_row.shape[0]
    def in_hbm(array):
        return pltpu.with_memory_space_constraint(array, pltpu.HBM)

    operands = (
        rhs, diag, smoother_center, smoother_faces,
        jnp.broadcast_to(send_count.reshape(8, 1), (8, BLK)),
        send_cell.reshape(8, cap), rows(restrict_col), rows(restrict_vals),
        rows(coarse_col), coarse_diag.reshape(-1, BLK), rows(coarse_vals),
        csmooth_diag.reshape(-1, BLK), rows(csmooth_vals),
        remote_row.reshape(ki, 8, cap), remote_vals.reshape(ki, 8, cap),
        interp_row, interp_vals,
    )
    shapes = {
        "rhs": rhs.shape, "send_cell": (8, cap), "restrict_col": operands[6].shape,
        "coarse_col": operands[8].shape, "interp_row": interp_row.shape,
    }
    sizes = (lax.axis_size("gx"), lax.axis_size("gy"))
    operands = [x if n == 4 else in_hbm(x) for n, x in enumerate(operands)]
    return make_kernel(sizes, shapes)(*operands)


def solution(mesh):
    fine = P("gx", "gy", None)
    listed = P(None, "gx", "gy", None)
    placed = (
        fine, fine, fine, listed, fine, P("gx", "gy", None, None), listed, listed,
        listed, fine, listed, fine, listed,
        P(None, "gx", "gy", None, None), P(None, "gx", "gy", None, None),
        listed, listed,
    )
    return jax.shard_map(
        body, mesh=mesh, in_specs=placed, out_specs=(fine, fine), check_vma=False
    )
```

```python
import jax
import jax.numpy as jnp
from jax import lax
from jax.experimental import pallas as pl
from jax.experimental.pallas import tpu as pltpu
from jax.sharding import PartitionSpec as P

BLK = 128
OFFSETS = ((-1, -1), (-1, 0), (-1, 1), (0, -1), (0, 1), (1, -1), (1, 0), (1, 1))
SIDES = ((-1, 0), (1, 0), (0, -1), (0, 1))
MESH_ID = pl.DeviceIdType.MESH


def split_two(table):
    high = table.astype(jnp.bfloat16)
    low = (table - high.astype(jnp.float32)).astype(jnp.bfloat16)
    return jnp.concatenate([high, low], axis=1)


def one_hot(base, width):
    ids = lax.broadcasted_iota(jnp.int32, (base.shape[0], width), 1)
    return jnp.where(ids == base, 1.0, 0.0).astype(jnp.bfloat16)


def pick(index, base, table_two):
    both = jnp.dot(
        one_hot(base, table_two.shape[0]), table_two, preferred_element_type=jnp.float32
    )
    rows = both[:, :BLK] + both[:, BLK:]
    return jnp.take_along_axis(rows, index & (BLK - 1), axis=1, mode="promise_in_bounds")


def make_kernel(sizes, shapes):
    na, nb = sizes
    cx, cy, nz = shapes["rhs"]
    zblocks = nz // BLK
    cells = cx * cy
    fine_rows = cells * zblocks
    cap = shapes["send_cell"][1]
    slots = cap // BLK
    kr, crows, _ = shapes["restrict_col"]
    ka = shapes["coarse_col"][0]
    ki = shapes["interp_row"][0]
    rim_rows = 8

    def fine_place(block):
        return (block % zblocks) * cells + block // zblocks

    def kernel(
        rhs_h, diag_h, center_h, faces_h, count_ref, cell_h, rcol_h, rval_h, ccol_h,
        cdiag_h, cval_h, mdiag_h, mval_h, rrow_h, rrval_h, irow_h, ival_h,
        sol_ref, res_ref,
        field, ysend, yrecv, diag, center, faces, cell, rcol, rval, ccol, cdiag, cval,
        mdiag, mval, rrow, rrval, irow, ival, resid, fine_two, choose, sent, received,
        back, returned, coarse, rim, spread, partial,
        in_sem, halo_send, halo_recv, slot_send, slot_recv, back_send, back_recv,
        rim_send, rim_recv,
    ):
        a = lax.axis_index("gx")
        b = lax.axis_index("gy")

        loads = [
            (rhs_h, field.at[0, pl.ds(1, cx)]), (center_h, center), (faces_h, faces),
            (diag_h, diag), (cell_h, cell), (rcol_h, rcol), (rval_h, rval),
            (ccol_h, ccol), (mdiag_h, mdiag), (mval_h, mval), (cdiag_h, cdiag),
            (cval_h, cval), (rrow_h, rrow), (rrval_h, rrval), (irow_h, irow),
            (ival_h, ival),
        ]
        loads = [
            pltpu.make_async_copy(source, target, in_sem.at[n])
            for n, (source, target) in enumerate(loads)
        ]
        for load in loads:
            load.start()

        def there(step):
            dx, dy = step
            checks = []
            if dx < 0:
                checks.append(a > 0)
            if dx > 0:
                checks.append(a < na - 1)
            if dy < 0:
                checks.append(b > 0)
            if dy > 0:
                checks.append(b < nb - 1)
            out = checks[0]
            for check in checks[1:]:
                out = jnp.logical_and(out, check)
            return out

        exists = [there(step) for step in OFFSETS]
        side_exists = [there(step) for step in SIDES]

        barrier = pltpu.get_barrier_semaphore()
        total = jnp.int32(0)
        for d, (dx, dy) in enumerate(OFFSETS):
            @pl.when(exists[d])
            def _():
                pl.semaphore_signal(
                    barrier, inc=1, device_id=(a + dx, b + dy), device_id_type=MESH_ID
                )
            total = total + exists[d].astype(jnp.int32)

        for s in range(4):
            @pl.when(jnp.logical_not(side_exists[s]))
            def _():
                for t in range(5):
                    if s < 2:
                        field[t, 0 if s == 0 else cx + 1] = jnp.zeros((cy, nz), jnp.float32)
                    else:
                        yrecv[t, s - 2] = jnp.zeros((cx, nz), jnp.float32)
        for d in range(8):
            @pl.when(jnp.logical_not(exists[d]))
            def _():
                received[d] = jnp.zeros((slots, BLK), jnp.float32)
                returned[d] = jnp.zeros((slots, BLK), jnp.float32)
                for t in range(3):
                    rim[t, d] = jnp.zeros((rim_rows, BLK), jnp.float32)

        def halo_copy(t, s):
            dx, dy = SIDES[s]
            if s == 0:
                src, dst = field.at[t, 1], field.at[t, cx + 1]
            elif s == 1:
                src, dst = field.at[t, cx], field.at[t, 0]
            else:
                src, dst = ysend.at[t, s - 2], yrecv.at[t, 3 - s]
            return pltpu.make_async_remote_copy(
                src_ref=src, dst_ref=dst, send_sem=halo_send.at[t, s],
                recv_sem=halo_recv.at[t, s ^ 1],
                device_id=(a + dx, b + dy), device_id_type=MESH_ID,
            )

        def halo_arrival(t, s):
            dx, dy = SIDES[s]
            dst = field.at[t, 0 if s == 0 else cx + 1] if s < 2 else yrecv.at[t, s - 2]
            return pltpu.make_async_remote_copy(
                src_ref=dst, dst_ref=dst, send_sem=halo_send.at[t, s],
                recv_sem=halo_recv.at[t, s],
                device_id=(a + dx, b + dy), device_id_type=MESH_ID,
            )

        def start_halo(t):
            for s in (2, 3, 0, 1):
                @pl.when(side_exists[s])
                def _():
                    halo_copy(t, s).start()

        def wait_halo(t):
            for s in range(4):
                @pl.when(side_exists[s])
                def _():
                    halo_arrival(t, s).wait_recv()

        def eight_copy(src, dst, send_sem, recv_sem, d):
            dx, dy = OFFSETS[d]
            return pltpu.make_async_remote_copy(
                src_ref=src(d), dst_ref=dst(7 - d), send_sem=send_sem(d),
                recv_sem=recv_sem(7 - d),
                device_id=(a + dx, b + dy), device_id_type=MESH_ID,
            )

        def eight_arrival(dst, send_sem, recv_sem, d):
            dx, dy = OFFSETS[d]
            return pltpu.make_async_remote_copy(
                src_ref=dst(d), dst_ref=dst(d), send_sem=send_sem(d), recv_sem=recv_sem(d),
                device_id=(a + dx, b + dy), device_id_type=MESH_ID,
            )

        slot_plan = (
            lambda d: sent.at[d], lambda d: received.at[d],
            lambda d: slot_send.at[d], lambda d: slot_recv.at[d],
        )
        back_plan = (
            lambda d: back.at[d], lambda d: returned.at[d],
            lambda d: back_send.at[d], lambda d: back_recv.at[d],
        )

        def rim_plan(t):
            return (
                lambda d: coarse.at[t, pl.ds(0, rim_rows)], lambda d: rim.at[t, d],
                lambda d: rim_send.at[t, d], lambda d: rim_recv.at[t, d],
            )

        def start_eight(plan):
            for d in (0, 2, 5, 7, 3, 4, 1, 6):
                @pl.when(exists[d])
                def _():
                    eight_copy(*plan, d).start()

        def wait_eight(plan):
            for d in range(8):
                @pl.when(exists[d])
                def _():
                    eight_arrival(*plan[1:], d).wait_recv()

        row_ids = lax.broadcasted_iota(jnp.int32, (cy, nz), 0)
        lane_ids = lax.broadcasted_iota(jnp.int32, (cy, nz), 1)

        zeros = jnp.zeros((cy, nz), jnp.float32)

        def beside(t, i):
            centre = field[t, i + 1]
            return centre, [
                field[t, i] if i > 0 else zeros,
                field[t, i + 2] if i < cx - 1 else zeros,
                jnp.where(row_ids == 0, 0.0, pltpu.roll(centre, 1, 0)),
                jnp.where(row_ids == cy - 1, 0.0, pltpu.roll(centre, cy - 1, 0)),
                jnp.where(lane_ids == 0, 0.0, pltpu.roll(centre, 1, 1)),
                jnp.where(lane_ids == nz - 1, 0.0, pltpu.roll(centre, nz - 1, 1)),
            ]

        def sides(t, i):
            out = [
                jnp.where(row_ids == 0, jnp.broadcast_to(yrecv[t, 0, i:i + 1, :], (cy, nz)), 0.0),
                jnp.where(row_ids == cy - 1, jnp.broadcast_to(yrecv[t, 1, i:i + 1, :], (cy, nz)), 0.0),
            ]
            return [
                field[t, 0] if i == 0 else None,
                field[t, cx + 1] if i == cx - 1 else None,
            ] + out

        def residual_inside(t):
            for i in range(cx):
                centre, near = beside(t, i)
                sums = near[0]
                for one in near[1:]:
                    sums = sums + one
                partial[i] = field[0, i + 1] - ((6.0 + diag[i]) * centre - sums)

        def residual_row(t, i):
            out = partial[i]
            for one in sides(t, i):
                if one is not None:
                    out = out + one
            return out

        def smoother_inside(t, base):
            for i in range(cx):
                centre, near = beside(t, i)
                out = center[i] * centre
                for q in range(6):
                    out = out + faces[q, i] * near[q]
                partial[i] = out if base is None else field[base, i + 1] + out

        def smoother_row(t, i):
            out = partial[i]
            for q, one in enumerate(sides(t, i)):
                if one is not None:
                    out = out + faces[q, i] * one
            return out

        def put(t, i, value):
            field[t, i + 1] = value
            ysend[t, 0, i:i + 1, :] = value[0:1]
            ysend[t, 1, i:i + 1, :] = value[cy - 1:cy]

        loads[0].wait()
        for i in range(cx):
            value = field[0, i + 1]
            ysend[0, 0, i:i + 1, :] = value[0:1]
            ysend[0, 1, i:i + 1, :] = value[cy - 1:cy]
        pl.semaphore_wait(barrier, total)
        start_halo(0)
        for load in loads[1:5]:
            load.wait()

        cell_index = jnp.concatenate(
            [cell[:, s * BLK:(s + 1) * BLK] for s in range(slots)], axis=0
        )
        cell_base = fine_place(cell_index[:, 0:1] // BLK)
        across = jnp.transpose(
            jnp.broadcast_to(cell_base, (8 * slots, BLK)).astype(jnp.float32)
        )[0:1].astype(jnp.int32)
        fine_ids = lax.broadcasted_iota(jnp.int32, (fine_rows, 8 * slots), 0)
        choose[...] = jnp.where(fine_ids == across, 1.0, 0.0).astype(jnp.bfloat16)

        smoother_inside(0, None)
        wait_halo(0)
        for i in range(cx):
            put(1, i, smoother_row(0, i))
        start_halo(1)
        residual_inside(1)
        for load in loads[5:]:
            load.wait()

        wait_halo(1)
        for i in range(cx):
            resid[i] = residual_row(1, i)
        table = jnp.concatenate(
            [resid[:, :, z * BLK:(z + 1) * BLK].reshape(cells, BLK) for z in range(zblocks)],
            axis=0,
        )
        fine_two[...] = split_two(table)

        picked = pick(cell_index, cell_base, fine_two[...])
        lanes = lax.broadcasted_iota(jnp.int32, (8, BLK), 1)
        for s in range(slots):
            live = lanes + s * BLK < count_ref[...]
            values = jnp.where(live, picked[8 * s:8 * s + 8], 0.0)
            for d in range(8):
                sent[d, s:s + 1, :] = values[d:d + 1]
        start_eight(slot_plan)

        step = 9 if kr % 9 == 0 else 1

        def restrict_some(c, acc):
            index = rcol[pl.ds(c * step, step)].reshape(step * crows, BLK)
            block = index[:, 0:1] // BLK
            base = jnp.where(block < fine_rows, fine_place(block), -1)
            got = pick(index, base, fine_two[...]).reshape(step, crows, BLK)
            return acc + jnp.sum(got * rval[pl.ds(c * step, step)], axis=0)

        rc = lax.fori_loop(
            0, kr // step, restrict_some, jnp.zeros((crows, BLK), jnp.float32)
        )
        wait_eight(slot_plan)
        received_two = split_two(received[...].reshape(8 * slots, BLK))
        index = rcol[:, 0:rim_rows, :].reshape(kr * rim_rows, BLK)
        got = pick(index, index[:, 0:1] // BLK - fine_rows, received_two)
        more = jnp.sum(
            got.reshape(kr, rim_rows, BLK) * rval[:, 0:rim_rows, :], axis=0
        )
        rc = jnp.concatenate([rc[:rim_rows] + more, rc[rim_rows:]], axis=0)

        def coarse_apply(t, vector, diagonal, values):
            coarse[t] = vector
            start_eight(rim_plan(t))
            index = ccol[...].reshape(ka * crows, BLK)
            got = pick(index, index[:, 0:1] // BLK, split_two(vector))
            own = diagonal[...] * vector + jnp.sum(
                got.reshape(ka, crows, BLK) * values[...], axis=0
            )
            wait_eight(rim_plan(t))
            index = ccol[:, 0:rim_rows, :].reshape(ka * rim_rows, BLK)
            got = pick(
                index, index[:, 0:1] // BLK - crows,
                split_two(rim[t].reshape(8 * rim_rows, BLK)),
            )
            more = jnp.sum(
                got.reshape(ka, rim_rows, BLK) * values[:, 0:rim_rows, :], axis=0
            )
            return jnp.concatenate([own[:rim_rows] + more, own[rim_rows:]], axis=0)

        xc1 = coarse_apply(0, rc, mdiag, mval)
        rc2 = rc - coarse_apply(1, xc1, cdiag, cval)
        xc2 = xc1 + coarse_apply(2, rc2, mdiag, mval)
        coarse_two = split_two(xc2)

        group = 8 if slots % 8 == 0 else 1
        for c in range(slots // group):
            parts = [(c * group + g) * BLK for g in range(group)]
            index = jnp.concatenate(
                [rrow[:, :, p:p + BLK].reshape(ki * 8, BLK) for p in parts], axis=0
            )
            got = pick(index, index[:, 0:1] // BLK, coarse_two)
            for g, p in enumerate(parts):
                mine = got[g * ki * 8:(g + 1) * ki * 8].reshape(ki, 8, BLK)
                values = jnp.sum(mine * rrval[:, :, p:p + BLK], axis=0)
                for d in range(8):
                    back[d, c * group + g:c * group + g + 1, :] = values[d:d + 1]
        start_eight(back_plan)

        for z in range(zblocks):
            p = z * BLK
            index = irow[:, :, :, p:p + BLK].reshape(ki * cells, BLK)
            got = pick(index, index[:, 0:1] // BLK, coarse_two)
            got = got.reshape(ki, cx, cy, BLK) * ival[:, :, :, p:p + BLK]
            field[2, 1:cx + 1, :, p:p + BLK] = (
                field[1, 1:cx + 1, :, p:p + BLK] + jnp.sum(got, axis=0)
            )
        wait_eight(back_plan)

        fold_rows = lax.broadcasted_iota(jnp.int32, (64, BLK), 0)
        fold_lanes = lax.broadcasted_iota(jnp.int32, (64, BLK), 1)
        fold_index = (fold_lanes % 16) * 8 + fold_rows % 8
        fold_keep = fold_lanes // 16 == fold_rows // 8

        def spread_some(s, carry):
            p = pl.multiple_of(s * BLK, BLK)
            values = jnp.concatenate(
                [returned[d, pl.ds(s, 1), :] for d in range(8)], axis=0
            )
            values = jnp.where(lanes + p < count_ref[...], values, 0.0)
            within = cell[:, pl.ds(p, BLK)] & (BLK - 1)
            upper, lower = within // 16, within % 16
            coarse_part = jnp.concatenate(
                [jnp.where(upper == h, values, 0.0) for h in range(8)], axis=0
            )
            high = coarse_part.astype(jnp.bfloat16)
            low = (coarse_part - high.astype(jnp.float32)).astype(jnp.bfloat16)
            fine_part = jnp.concatenate(
                [jnp.where(lower == l, 1.0, 0.0) for l in range(16)], axis=0
            ).astype(jnp.bfloat16)
            out = lax.dot_general(
                jnp.concatenate([high, low], axis=0), fine_part,
                (((1,), (1,)), ((), ())), preferred_element_type=jnp.float32,
            )
            out = jnp.take_along_axis(
                out[:64] + out[64:], fold_index, axis=1, mode="promise_in_bounds"
            )
            out = jnp.where(fold_keep, out, 0.0).reshape(8, 8, BLK)
            spread[pl.ds(pl.multiple_of(s * 8, 8), 8)] = jnp.sum(out, axis=0)
            return carry

        lax.fori_loop(0, slots, spread_some, 0, unroll=32)
        both = jnp.dot(
            choose[...], split_two(spread[...]), preferred_element_type=jnp.float32
        )
        added = both[:, :BLK] + both[:, BLK:]
        for z in range(zblocks):
            p = z * BLK
            field[2, 1:cx + 1, :, p:p + BLK] = (
                field[2, 1:cx + 1, :, p:p + BLK]
                + added[z * cells:(z + 1) * cells].reshape(cx, cy, BLK)
            )
        for i in range(cx):
            value = field[2, i + 1]
            ysend[2, 0, i:i + 1, :] = value[0:1]
            ysend[2, 1, i:i + 1, :] = value[cy - 1:cy]
        start_halo(2)
        residual_inside(2)
        wait_halo(2)

        for i in range(cx):
            put(3, i, residual_row(2, i))
        start_halo(3)
        smoother_inside(3, 2)
        wait_halo(3)
        for i in range(cx):
            value = smoother_row(3, i)
            put(4, i, value)
            sol_ref[i] = value
        start_halo(4)
        residual_inside(4)
        wait_halo(4)
        for i in range(cx):
            res_ref[i] = residual_row(4, i)

        for t in range(5):
            for s in range(4):
                @pl.when(side_exists[s])
                def _():
                    halo_copy(t, s).wait_send()
        for plan in (slot_plan, back_plan, rim_plan(0), rim_plan(1), rim_plan(2)):
            for d in range(8):
                @pl.when(exists[d])
                def _():
                    eight_copy(*plan, d).wait_send()

    f32, i32, bf16 = jnp.float32, jnp.int32, jnp.bfloat16
    vm = pltpu.VMEM
    dma = pltpu.SemaphoreType.DMA
    scratch = [
        vm((5, cx + 2, cy, nz), f32), vm((5, 2, cx, nz), f32), vm((5, 2, cx, nz), f32),
        vm((cx, cy, nz), f32), vm((cx, cy, nz), f32), vm((6, cx, cy, nz), f32),
        vm((8, cap), i32), vm((kr, crows, BLK), i32), vm((kr, crows, BLK), f32),
        vm((ka, crows, BLK), i32), vm((crows, BLK), f32), vm((ka, crows, BLK), f32),
        vm((crows, BLK), f32), vm((ka, crows, BLK), f32),
        vm((ki, 8, cap), i32), vm((ki, 8, cap), f32),
        vm((ki, cx, cy, nz), i32), vm((ki, cx, cy, nz), f32),
        vm((cx, cy, nz), f32), vm((fine_rows, 2 * BLK), bf16),
        vm((fine_rows, 8 * slots), bf16),
        vm((8, slots, BLK), f32), vm((8, slots, BLK), f32),
        vm((8, slots, BLK), f32), vm((8, slots, BLK), f32),
        vm((3, crows, BLK), f32), vm((3, 8, rim_rows, BLK), f32),
        vm((8 * slots, BLK), f32), vm((cx, cy, nz), f32),
        dma((16,)), dma((5, 4)), dma((5, 4)), dma((8,)), dma((8,)), dma((8,)), dma((8,)),
        dma((3, 8)), dma((3, 8)),
    ]
    whole = pl.BlockSpec(memory_space=pltpu.VMEM)
    in_hbm = pl.BlockSpec(memory_space=pltpu.HBM)
    return pl.pallas_call(
        kernel,
        out_shape=(
            jax.ShapeDtypeStruct((cx, cy, nz), f32),
            jax.ShapeDtypeStruct((cx, cy, nz), f32),
        ),
        in_specs=[in_hbm] * 4 + [whole] + [in_hbm] * 12,
        out_specs=(whole, whole),
        scratch_shapes=scratch,
        compiler_params=pltpu.CompilerParams(
            collective_id=0, has_side_effects=True, vmem_limit_bytes=40 * 1024 * 1024
        ),
        name="vcycle",
    )


def body(
    rhs, diag, smoother_center, smoother_faces, send_count, send_cell, restrict_col,
    restrict_vals, coarse_col, coarse_diag, coarse_vals, csmooth_diag, csmooth_vals,
    remote_row, remote_vals, interp_row, interp_vals,
):
    def rows(array):
        return array.reshape(array.shape[0], -1, BLK)

    cap = send_cell.shape[-1]
    ki = remote_row.shape[0]
    def in_hbm(array):
        return pltpu.with_memory_space_constraint(array, pltpu.HBM)

    operands = (
        rhs, diag, smoother_center, smoother_faces,
        jnp.broadcast_to(send_count.reshape(8, 1), (8, BLK)),
        send_cell.reshape(8, cap), rows(restrict_col), rows(restrict_vals),
        rows(coarse_col), coarse_diag.reshape(-1, BLK), rows(coarse_vals),
        csmooth_diag.reshape(-1, BLK), rows(csmooth_vals),
        remote_row.reshape(ki, 8, cap), remote_vals.reshape(ki, 8, cap),
        interp_row, interp_vals,
    )
    shapes = {
        "rhs": rhs.shape, "send_cell": (8, cap), "restrict_col": operands[6].shape,
        "coarse_col": operands[8].shape, "interp_row": interp_row.shape,
    }
    sizes = (lax.axis_size("gx"), lax.axis_size("gy"))
    operands = [x if n == 4 else in_hbm(x) for n, x in enumerate(operands)]
    return make_kernel(sizes, shapes)(*operands)


def solution(mesh):
    fine = P("gx", "gy", None)
    listed = P(None, "gx", "gy", None)
    placed = (
        fine, fine, fine, listed, fine, P("gx", "gy", None, None), listed, listed,
        listed, fine, listed, fine, listed,
        P(None, "gx", "gy", None, None), P(None, "gx", "gy", None, None),
        listed, listed,
    )
    return jax.shard_map(
        body, mesh=mesh, in_specs=placed, out_specs=(fine, fine), check_vma=False
    )
```
